256 devices in a mesh: seq: 32 (over y, x, core), chan: 8 (over z).
Axes of the slice: x: 4, y: 4, z: 8, core: 2. Of those that a mesh axis runs over, the one named last changes fastest.
Arguments:
- tokens: bfloat16 [8192, 4096], P('seq', 'chan'), may hold values from -6 to 6
- input_weight: bfloat16 [3, 4096, 4096], P(None, 'seq', 'chan'), may hold values from -0.09375 to 0.09375
- short_taps: float32 [3, 3, 4096], P(None, None, 'chan'), may hold values from -3 to 3
- residue: float32 [16, 4096], P(None, 'chan'), may hold values from -1.5 to 1.5
- decay_rate: float32 [16, 4096], P(None, 'chan'), may hold values from 0.1 to 409
- out_weight: bfloat16 [4096, 4096], P('chan'), may hold values from -0.125 to 0.125
Outputs:
- hyena_out: bfloat16 [8192, 4096], P('seq', 'chan')
The draws below stay inside these ranges and needn't reach their ends.
All inputs are finite; a program needn't handle non-finite values.
Results may differ from the reference program's by a relative error of at most 0.025.
Values may be sent and summed in bfloat16 or wider, within the bound.
No kernel may reach another device: no remote copies, remote signals or barrier semaphores. Data moves between devices by JAX's collectives and lax.ppermute only.
A program may use at most 128 MiB of HBM per device.

```python
import math
import jax
import jax.numpy as jnp
from jax import lax

C = 4096
MODES = 16
KS = 3
L = 8192
N_CHAN = 8


def spiked(values, own_key, source, target, shards_of, factor):
    def block_of(dim):
        return (jnp.arange(values.shape[dim]) // (values.shape[dim] // shards_of)).reshape((-1,) + (1,) * (values.ndim - 1 - dim))

    first = jax.random.permutation(own_key, shards_of)[block_of(target)]
    second = (block_of(target) + shards_of // 2) % shards_of
    return jnp.where((block_of(source) == first) | (block_of(source) == second), factor * values, values)


def levels(key, extent, cuts, least, high):
    def one(position, shards_of):
        steps = jax.random.uniform(jax.random.fold_in(jax.random.fold_in(key, 6), position), (shards_of,), jnp.float32, least / len(cuts), high / len(cuts))
        return jnp.repeat(jnp.exp(steps), extent[position] // shards_of).reshape((-1,) + (1,) * (len(extent) - position - 1))

    gain = one(*cuts[0])
    for cut in cuts[1:]:
        gain = gain * one(*cut)
    return gain


def normal_values(stream_key, shape, scale, most, cuts=(), kind=jnp.bfloat16):
    level = levels(stream_key, shape, cuts, -0.22, 0.18) if cuts else 1.0
    values = jax.random.normal(stream_key, shape, jnp.float32) * scale * level
    return jnp.minimum(jnp.maximum(values, -most), most).astype(kind)


def bell_draw_with(key, extent, scale, most, pieces, heavy, kind=jnp.bfloat16):
    result = scale * jax.random.normal(key, extent, jnp.float32)
    if pieces:
        result = result * levels(key, extent, pieces, -0.22, 0.18)
    return jnp.clip(spiked(result, jax.random.fold_in(key, 3), *heavy), -most, most).astype(kind)


def setup_inputs(seed: int = 0) -> dict:
    streams_of = jax.random.split(jax.random.key(seed), 7)
    tokens = normal_values(streams_of[0], (L, C), 1.0, 6.0, ((0, 32), (1, 8)))
    input_weight = normal_values(streams_of[1], (3, C, C), C ** -0.5, 0.09375, ((1, 32), (2, 8)))
    short_taps = normal_values(streams_of[2], (3, KS, C), 0.5, 3.0, ((2, 8),), jnp.float32)
    residue = normal_values(streams_of[3], (MODES, C), 0.25, 1.5, ((1, 8),), jnp.float32)
    decay_rate = jnp.clip(jnp.exp(math.log(409.0) - 8.3163 * jax.random.uniform(streams_of[4], (MODES, C), jnp.float32) ** levels(streams_of[4], (MODES, C), ((1, 8),), -0.2, 0.2)), 0.1, 409.0)
    out_weight = bell_draw_with(streams_of[5], (C, C), C ** -0.5, 0.125, ((0, 8),), (0, 1, 8, 2.0))
    return {"tokens": tokens, "input_weight": input_weight, "short_taps": short_taps, "residue": residue, "decay_rate": decay_rate, "out_weight": out_weight}


def reference(tokens, input_weight, short_taps, residue, decay_rate, out_weight):
    projected_input = jnp.einsum('rh,phv->prv', tokens.astype(jnp.float32), input_weight.astype(jnp.float32)).astype(jnp.bfloat16)
    zero_rows = jnp.zeros((3, 2, C), jnp.bfloat16)
    extended = jnp.concatenate([zero_rows, projected_input], axis=1).astype(jnp.float32)
    tap_weights = short_taps[:, :, None, :]
    filtered = tap_weights[:, 0] * extended[:, 2:] + tap_weights[:, 1] * extended[:, 1:-1] + tap_weights[:, 2] * extended[:, :-2]
    signal = filtered[1] * filtered[2]
    rates = decay_rate / L
    amplitude = residue * jnp.sqrt(-jnp.expm1(-2.0 * rates))
    block_extent = min(C, 128)
    block_count = C // block_extent
    positions = jnp.arange(L, dtype=jnp.int32).astype(jnp.float32)

    def convolve(operands):
        signal_block, rate_block, amp_block = operands
        kernel = jnp.zeros_like(signal_block)
        for number in range(MODES):
            kernel = kernel + amp_block[number][None, :] * jnp.exp(-rate_block[number][None, :] * positions[:, None])
        spectrum = jnp.fft.rfft(signal_block, n=2 * L, axis=0) * jnp.fft.rfft(kernel, n=2 * L, axis=0)
        return jnp.fft.irfft(spectrum, n=2 * L, axis=0)[:L]
    convolved = lax.map(convolve, (signal.reshape(L, block_count, block_extent).transpose(1, 0, 2), rates.reshape(MODES, block_count, block_extent).transpose(1, 0, 2), amplitude.reshape(MODES, block_count, block_extent).transpose(1, 0, 2)))
    convolved = convolved.transpose(1, 0, 2).reshape(L, C)
    gated = (filtered[0] * convolved).astype(jnp.bfloat16)
    group_width = C // N_CHAN
    summed = jnp.zeros((L, C), jnp.float32)
    for group in range(N_CHAN):
        partial_sum = jnp.dot(gated[:, group * group_width:(group + 1) * group_width], out_weight[group * group_width:(group + 1) * group_width], preferred_element_type=jnp.float32).astype(jnp.bfloat16)
        partial_sum = lax.optimization_barrier(partial_sum)
        summed = summed + partial_sum.astype(jnp.float32)
    return summed.astype(jnp.bfloat16)
```

```python
import functools

import jax
import jax.numpy as jnp
from jax import lax
from jax.experimental import pallas as pl
from jax.experimental.pallas import tpu as pltpu
from jax.sharding import Mesh, PartitionSpec as P

HALO = 16
VMEM_LIMIT = 40 * 1024 * 1024


def shift(block, axis, distance):
    n = lax.axis_size(axis)
    return lax.ppermute(block, axis, [(i, (i + distance) % n) for i in range(n)])


def shift_open(block, axis, distance):
    n = lax.axis_size(axis)
    return lax.ppermute(block, axis, [(i, i + distance) for i in range(n - distance)])


def swap_cores(block):
    return lax.ppermute(block, "core", [(0, 1), (1, 0)])


def tokens_around(tokens):
    half = tokens.shape[1] // 2
    parts = [(0, 0, tokens)]
    right = left = tokens
    for step in (1, 2, 3):
        right = shift(right, "chan", 1)
        left = shift(left, "chan", -1)
        parts.append((-step, 0, right))
        parts.append((step, 0, left))
    parts.append((4, 0, shift(right[:, :half], "chan", 1)))
    parts.append((4, half, shift(left[:, half:], "chan", -1)))
    return parts


def accumulate(layout, groups, place, mine, partner, weight, sum_mine, sum_partner):
    group_rows = weight.shape[0] // groups
    for number, (offset, first) in enumerate(layout):
        depth = mine[number].shape[1]
        group = lax.rem(place[0] + offset + groups, groups)
        start = pl.multiple_of(group * group_rows + first, 128)
        rows = weight[pl.ds(start, depth), :]
        for tokens, total in ((mine[number], sum_mine), (partner[number], sum_partner)):
            product = jnp.dot(tokens[...], rows, preferred_element_type=jnp.float32)
            if number == 0:
                total[...] = product
            else:
                total[...] += product


def in_order(place, sum_mine, sum_partner, projected):
    rows = sum_mine.shape[0]
    step = rows - HALO
    mine = pl.multiple_of(place[1] * step, 16)
    partner = pl.multiple_of((1 - place[1]) * step, 16)
    projected[pl.ds(mine, rows), :] = sum_mine[...].astype(jnp.bfloat16).astype(jnp.float32)
    projected[pl.ds(partner, rows), :] = sum_partner[...].astype(jnp.bfloat16).astype(jnp.float32)


def filtered(projected, taps, group, channels, columns):
    rows = projected.shape[0] - HALO
    return sum(
        taps[group, lag : lag + 1, channels] * projected[pl.ds(HALO - lag, rows), columns]
        for lag in range(taps.shape[1])
    )


def key_value_kernel(layout, groups, place, *refs):
    n = len(layout)
    mine, partner = refs[:n], refs[n : 2 * n]
    weight, taps, rates, signal, block_ends, end_state, sum_mine, sum_partner, projected = refs[2 * n :]
    accumulate(layout, groups, place, mine, partner, weight, sum_mine, sum_partner)
    in_order(place, sum_mine, sum_partner, projected)
    modes, blocks, width = block_ends.shape
    steps = signal.shape[1] // blocks
    for part in range(width // 128):
        lanes = pl.ds(part * 128, 128)
        key = filtered(projected, taps, 1, lanes, lanes)
        value = filtered(projected, taps, 2, lanes, pl.ds(width + part * 128, 128))
        signal[part] = key * value
        decay = [
            jnp.broadcast_to(jnp.exp(-rates[m : m + 1, lanes]), (blocks, 128)) for m in range(modes)
        ]

        def step(s, states):
            u = signal[part, pl.ds(s, blocks, steps), :]
            return tuple(decay[m] * states[m] + u for m in range(modes))

        zero = jnp.zeros((blocks, 128), jnp.float32)
        states = lax.fori_loop(0, steps, step, (zero,) * modes, unroll=8)
        for m in range(modes):
            block_ends[m, :, lanes] = states[m]
    block_decay = jnp.exp(-rates[...] * float(steps))
    state = block_ends[:, 0, :]
    for b in range(1, blocks):
        state = block_decay * state + block_ends[:, b, :]
    end_state[...] = state


def query_kernel(layout, groups, place, *refs):
    n = len(layout)
    mine, partner = refs[:n], refs[n : 2 * n]
    weight, taps, query, sum_mine, sum_partner, projected = refs[2 * n :]
    accumulate(layout, groups, place, mine, partner, weight, sum_mine, sum_partner)
    in_order(place, sum_mine, sum_partner, projected)
    query[...] = filtered(projected, taps, 0, slice(None), slice(None))


def scan_kernel(signal, query, block_ends, start_state, rates, amplitude, gated, block_starts, result):
    modes, blocks, width = block_ends.shape
    steps = signal.shape[1] // blocks
    block_decay = jnp.exp(-rates[...] * float(steps))
    state = start_state[...]
    for b in range(blocks):
        block_starts[:, b, :] = state
        state = block_decay * state + block_ends[:, b, :]
    for part in range(width // 128):
        lanes = pl.ds(part * 128, 128)
        decay = [
            jnp.broadcast_to(jnp.exp(-rates[m : m + 1, lanes]), (blocks, 128)) for m in range(modes)
        ]
        scale = [jnp.broadcast_to(amplitude[m : m + 1, lanes], (blocks, 128)) for m in range(modes)]

        def step(s, states):
            u = signal[part, pl.ds(s, blocks, steps), :]
            states = tuple(decay[m] * states[m] + u for m in range(modes))
            terms = [scale[m] * states[m] for m in range(modes)]
            while len(terms) > 1:
                terms = [a + b for a, b in zip(terms[::2], terms[1::2])]
            result[part, pl.ds(s, blocks, steps), :] = terms[0]
            return states

        states = tuple(block_starts[m, :, lanes] for m in range(modes))
        lax.fori_loop(0, steps, step, states, unroll=4)
        gated[:, lanes] = (query[:, lanes] * result[part]).astype(jnp.bfloat16)


def on_device(kernel, outs, scratch, cost, *arrays):
    smem = pl.BlockSpec(memory_space=pltpu.SMEM)
    vmem = pl.BlockSpec(memory_space=pltpu.VMEM)
    return pl.pallas_call(
        kernel,
        out_shape=outs,
        in_specs=[smem if a.dtype == jnp.int32 else vmem for a in arrays],
        out_specs=jax.tree.map(lambda _: vmem, outs),
        scratch_shapes=[pltpu.VMEM(s, jnp.float32) for s in scratch],
        compiler_params=pltpu.CompilerParams(vmem_limit_bytes=VMEM_LIMIT),
        cost_estimate=pl.CostEstimate(flops=cost, bytes_accessed=cost // 400, transcendentals=0),
    )(*arrays)


def carried_in(end_state, rates, positions):
    nx, ny = lax.axis_size("x"), lax.axis_size("y")
    x, y = lax.axis_index("x"), lax.axis_index("y")
    from_x = [end_state] + [shift(end_state, "x", d) for d in range(1, nx)]
    prefix = jnp.zeros_like(end_state)
    row_total = jnp.zeros_like(end_state)
    for d, state in enumerate(from_x):
        source = (x - d) % nx
        row_total += jnp.exp(-rates * (positions * (nx - 1 - source)).astype(jnp.float32)) * state
        if d:
            weight = jnp.exp(-rates * float(positions * (d - 1)))
            prefix += jnp.where(d <= x, weight * state, 0.0)
    from_y = [shift_open(row_total, "y", d) for d in range(1, ny)]
    above = jnp.zeros_like(end_state)
    for d, state in enumerate(from_y, 1):
        above += jnp.exp(-rates * float(positions * nx * (d - 1))) * state
    return prefix + jnp.exp(-rates * (positions * x).astype(jnp.float32)) * above


def shards(tokens, input_weight, short_taps, residue, decay_rate, out_weight):
    f32, bf16 = jnp.float32, jnp.bfloat16
    rows, _ = tokens.shape
    width = input_weight.shape[2] // 2
    groups = lax.axis_size("chan")
    core = lax.axis_index("core")
    chips = lax.axis_size("x") * lax.axis_size("y")
    positions = 2 * rows
    sequence = positions * chips
    place = jnp.stack([lax.axis_index("chan"), core]).astype(jnp.int32)

    def own_columns(array, owner):
        return lax.dynamic_slice_in_dim(array, owner * width, width, axis=array.ndim - 1)

    kept = own_columns(input_weight, core)
    got = swap_cores(own_columns(input_weight, 1 - core))
    both = jnp.where(core == 0, jnp.stack([kept, got]), jnp.stack([got, kept]))
    query_part = both[:, 0].reshape(-1, width)
    key_value_part = jnp.concatenate([both[:, 1], both[:, 2]], axis=-1).reshape(-1, 2 * width)
    key_value_weight = lax.all_gather(key_value_part, ("y", "x"), axis=0, tiled=True)
    query_part, _ = lax.optimization_barrier((query_part, key_value_weight[:16, :128]))
    query_weight = lax.all_gather(query_part, ("y", "x"), axis=0, tiled=True)

    last_rows = tokens[-HALO:]
    devices = range(2 * chips)
    earlier = lax.ppermute(last_rows, ("y", "x", "core"), [(i, i + 1) for i in devices[:-1]])
    parts = tokens_around(jnp.concatenate([earlier, tokens], axis=0))
    layout = tuple((offset, first) for offset, first, _ in parts)
    mine = [block for _, _, block in parts]
    partner = [swap_cores(block) for block in mine]

    rates_all = decay_rate / float(sequence)
    rates = own_columns(rates_all, core)
    amplitude = own_columns(residue * jnp.sqrt(-jnp.expm1(-2.0 * rates_all)), core)
    taps = own_columns(short_taps, core)
    modes = rates.shape[0]
    blocks = 8

    ext = rows + HALO
    signal, block_ends, end_state = on_device(
        functools.partial(key_value_kernel, layout, groups),
        (
            jax.ShapeDtypeStruct((width // 128, positions, 128), f32),
            jax.ShapeDtypeStruct((modes, blocks, width), f32),
            jax.ShapeDtypeStruct((modes, width), f32),
        ),
        ((ext, 2 * width), (ext, 2 * width), (positions + HALO, 2 * width)),
        2 * positions * key_value_weight.size,
        place, *mine, *partner, key_value_weight, taps, rates,
    )
    start_state = carried_in(end_state, rates, positions)
    query = on_device(
        functools.partial(query_kernel, layout, groups),
        jax.ShapeDtypeStruct((positions, width), f32),
        ((ext, width), (ext, width), (positions + HALO, width)),
        2 * positions * query_weight.size,
        place, *mine, *partner, query_weight, taps,
    )
    gated = on_device(
        scan_kernel,
        jax.ShapeDtypeStruct((positions, width), bf16),
        ((modes, blocks, width), (width // 128, positions, 128)),
        4 * modes * positions * width,
        signal, query, block_ends, start_state, rates, amplitude,
    )

    own = lax.dynamic_slice_in_dim(gated, core * rows, rows, axis=0)
    other = swap_cores(lax.dynamic_slice_in_dim(gated, (1 - core) * rows, rows, axis=0))
    ordered = jnp.where(
        core == 0, jnp.concatenate([own, other], axis=1), jnp.concatenate([other, own], axis=1)
    )
    partial_sum = jnp.dot(ordered, out_weight, preferred_element_type=f32)
    return lax.psum_scatter(
        partial_sum.astype(bf16), "chan", scatter_dimension=1, tiled=True
    )


def solution(mesh):
    devices = mesh.devices.reshape(4, 4, 2, 8)
    chips = Mesh(devices, ("y", "x", "core", "chan"))
    seq = ("y", "x", "core")
    placed = (
        P(seq, "chan"),
        P(None, seq, "chan"),
        P(None, None, "chan"),
        P(None, "chan"),
        P(None, "chan"),
        P("chan", None),
    )
    return jax.shard_map(
        shards, mesh=chips, in_specs=placed, out_specs=P(seq, "chan"), check_vma=False
    )
```

```python
import functools

import jax
import jax.numpy as jnp
from jax import lax
from jax.experimental import pallas as pl
from jax.experimental.pallas import tpu as pltpu
from jax.sharding import Mesh, PartitionSpec as P

HALO = 16
VMEM_LIMIT = 40 * 1024 * 1024


def shift(block, axis, distance):
    n = lax.axis_size(axis)
    return lax.ppermute(block, axis, [(i, (i + distance) % n) for i in range(n)])


def shift_open(block, axis, distance):
    n = lax.axis_size(axis)
    return lax.ppermute(block, axis, [(i, i + distance) for i in range(n - distance)])


def swap_cores(block):
    return lax.ppermute(block, "core", [(0, 1), (1, 0)])


def chip_ring(block, sides, stage, sign):
    ny, nx = sides
    pairs = []
    for y in range(ny):
        for x in range(nx):
            for c in range(2):
                to = (y, (x + sign) % nx) if c == stage else ((y + sign) % ny, x)
                pairs.append(((y * nx + x) * 2 + c, (to[0] * nx + to[1]) * 2 + c))
    return lax.ppermute(block, ("y", "x", "core"), pairs)


def group_ring(block):
    n = lax.axis_size("chan")
    pairs = []
    for c in range(2):
        for z in range(n):
            pairs.append((c * n + z, c * n + (z + 1 - 2 * c) % n))
    return lax.ppermute(block, ("core", "chan"), pairs)


def weights_around(block, sides):
    def ring(own, stage):
        half = own.shape[0] // 2
        before = chip_ring(own, sides, stage, 1)
        behind = chip_ring(own, sides, stage, -1)
        far = chip_ring(before[:half], sides, stage, 1), chip_ring(behind[half:], sides, stage, -1)
        return before, behind, far

    before, behind, far = ring(block, 0)
    near = jnp.concatenate([block, before, *far, behind], axis=0)
    before, behind, far = ring(near, 1)
    return near, before, behind, *far


def tokens_around(block, core):
    blocks = [block]
    for _ in range(3):
        blocks.append(group_ring(blocks[-1]))
    half = block.shape[1] // 2
    blocks.append(group_ring(lax.dynamic_slice_in_dim(blocks[-1], core * half, half, axis=1)))
    return blocks[1:]


def tokens_in_order(place, groups, streams, gathered, semaphores):
    copies = []
    core = place[1]
    ahead = 1 - 2 * core
    row = 0
    for own, mine, partner in streams:
        rows, depth = own.shape
        half = depth // 2
        for distance in range(5):
            for side, blocks in ((-1, mine), (1, partner)):
                if distance == 0 and side == 1:
                    continue
                block = own if distance == 0 else blocks[distance - 1]
                group = lax.rem(place[0] + side * ahead * distance + groups, groups)
                column = group * depth
                if distance == 4:
                    column = column + (core if side == -1 else 1 - core) * half
                column = pl.multiple_of(column, 128)
                copies.append(
                    pltpu.make_async_copy(
                        block,
                        gathered.at[pl.ds(row, rows), pl.ds(column, block.shape[1])],
                        semaphores.at[len(copies)],
                    )
                )
        row += rows
    for copy in copies:
        copy.start()
    return copies


def weights_in_order(place, sides, blocks, gathered, semaphores):
    ny, nx = sides
    core, y, x = place[1], place[2], place[3]
    near, before, behind, far_top, far_bottom = blocks
    rows = near.shape[0] // 4
    order = (0, -1, -2, 1)
    pieces = [(near, i, first, 0) for i, first in enumerate(order)]
    pieces += [(before, i, first, -1) for i, first in enumerate(order)]
    pieces += [(behind, i, first, 1) for i, first in enumerate(order)]
    pieces += [(far_top, i, order[i], -2) for i in range(2)]
    pieces += [(far_bottom, i, order[i + 2], -2) for i in range(2)]
    copies = []
    for block, i, first, second in pieces:
        dx = jnp.where(core == 0, first, second)
        dy = jnp.where(core == 0, second, first)
        chip = lax.rem(y + dy + ny, ny) * nx + lax.rem(x + dx + nx, nx)
        to = pl.multiple_of(chip * rows, 128)
        copies.append(
            pltpu.make_async_copy(
                block.at[pl.ds(i * rows, rows)],
                gathered.at[pl.ds(to, rows)],
                semaphores.at[len(copies)],
            )
        )
    for copy in copies:
        copy.start()
    return copies


def take_tokens(refs):
    return [(refs[i], refs[i + 1 : i + 5], refs[i + 5 : i + 9]) for i in (0, 9)]


def project(tokens, weight, depth, projected):
    total = None
    rows = tokens.shape[0] - HALO
    for first in range(0, tokens.shape[1], depth):
        part = pl.ds(first, depth)
        product = jnp.dot(tokens[:, part], weight[part, :], preferred_element_type=jnp.float32)
        total = product if total is None else total + product
    total = total.astype(jnp.bfloat16).astype(jnp.float32)
    projected[pl.ds(0, HALO), :] = total[rows:]
    projected[pl.ds(HALO, rows), :] = total[:rows]


def filtered(projected, taps, group, channels, columns):
    rows = projected.shape[0] - HALO
    return sum(
        taps[group, lag : lag + 1, channels] * projected[pl.ds(HALO - lag, rows), columns]
        for lag in range(taps.shape[1])
    )


def key_value_kernel(groups, sides, place, *refs):
    streams, weights = take_tokens(refs[:18]), refs[18:23]
    taps, rates, signal, block_ends, end_state, tokens, weight, projected, *semaphores = refs[23:]
    copies = weights_in_order(place, sides, weights, weight, semaphores[0])
    copies += tokens_in_order(place, groups, streams, tokens, semaphores[1])
    for copy in copies:
        copy.wait()
    project(tokens, weight, tokens.shape[1], projected)
    modes, blocks, width = block_ends.shape
    steps = signal.shape[1] // blocks
    for part in range(width // 128):
        lanes = pl.ds(part * 128, 128)
        key = filtered(projected, taps, 1, lanes, lanes)
        value = filtered(projected, taps, 2, lanes, pl.ds(width + part * 128, 128))
        signal[part] = key * value
        decay = [
            jnp.broadcast_to(jnp.exp(-rates[m : m + 1, lanes]), (blocks, 128)) for m in range(modes)
        ]

        def step(s, states):
            u = signal[part, pl.ds(s, blocks, steps), :]
            return tuple(decay[m] * states[m] + u for m in range(modes))

        zero = jnp.zeros((blocks, 128), jnp.float32)
        states = lax.fori_loop(0, steps, step, (zero,) * modes, unroll=8)
        for m in range(modes):
            block_ends[m, :, lanes] = states[m]
    block_decay = jnp.exp(-rates[...] * float(steps))
    state = block_ends[:, 0, :]
    for b in range(1, blocks):
        state = block_decay * state + block_ends[:, b, :]
    end_state[...] = state


def query_kernel(groups, place, *refs):
    streams = take_tokens(refs[:18])
    weight, taps, query, tokens, projected, semaphores = refs[18:]
    for copy in tokens_in_order(place, groups, streams, tokens, semaphores):
        copy.wait()
    project(tokens, weight, tokens.shape[1], projected)
    query[...] = filtered(projected, taps, 0, slice(None), slice(None))


def scan_kernel(signal, query, block_ends, start_state, rates, amplitude, gated, block_starts, result):
    modes, blocks, width = block_ends.shape
    steps = signal.shape[1] // blocks
    block_decay = jnp.exp(-rates[...] * float(steps))
    state = start_state[...]
    for b in range(blocks):
        block_starts[:, b, :] = state
        state = block_decay * state + block_ends[:, b, :]
    for part in range(width // 128):
        lanes = pl.ds(part * 128, 128)
        decay = [
            jnp.broadcast_to(jnp.exp(-rates[m : m + 1, lanes]), (blocks, 128)) for m in range(modes)
        ]
        scale = [jnp.broadcast_to(amplitude[m : m + 1, lanes], (blocks, 128)) for m in range(modes)]

        def step(s, states):
            u = signal[part, pl.ds(s, blocks, steps), :]
            states = tuple(decay[m] * states[m] + u for m in range(modes))
            terms = [scale[m] * states[m] for m in range(modes)]
            while len(terms) > 1:
                terms = [a + b for a, b in zip(terms[::2], terms[1::2])]
            result[part, pl.ds(s, blocks, steps), :] = terms[0]
            return states

        states = tuple(block_starts[m, :, lanes] for m in range(modes))
        lax.fori_loop(0, steps, step, states, unroll=4)
        gated[:, lanes] = (query[:, lanes] * result[part]).astype(jnp.bfloat16)


def on_device(kernel, outs, scratch, cost, places, *arrays):
    smem = pl.BlockSpec(memory_space=pltpu.SMEM)
    vmem = pl.BlockSpec(memory_space=pltpu.VMEM)
    anywhere = pl.BlockSpec(memory_space=pl.ANY)
    specs = [vmem] * len(arrays)
    if places:
        specs[: places + 1] = [smem] + [anywhere] * places
    return pl.pallas_call(
        kernel,
        out_shape=outs,
        in_specs=specs,
        out_specs=jax.tree.map(lambda _: vmem, outs),
        scratch_shapes=scratch,
        compiler_params=pltpu.CompilerParams(vmem_limit_bytes=VMEM_LIMIT),
        cost_estimate=pl.CostEstimate(flops=cost, bytes_accessed=cost // 400, transcendentals=0),
    )(*arrays)


def carried_in(end_state, rates, positions):
    nx, ny = lax.axis_size("x"), lax.axis_size("y")
    x, y = lax.axis_index("x"), lax.axis_index("y")
    from_x = [end_state] + [shift(end_state, "x", d) for d in range(1, nx)]
    prefix = jnp.zeros_like(end_state)
    row_total = jnp.zeros_like(end_state)
    for d, state in enumerate(from_x):
        source = (x - d) % nx
        row_total += jnp.exp(-rates * (positions * (nx - 1 - source)).astype(jnp.float32)) * state
        if d:
            weight = jnp.exp(-rates * float(positions * (d - 1)))
            prefix += jnp.where(d <= x, weight * state, 0.0)
    from_y = [shift_open(row_total, "y", d) for d in range(1, ny)]
    above = jnp.zeros_like(end_state)
    for d, state in enumerate(from_y, 1):
        above += jnp.exp(-rates * float(positions * nx * (d - 1))) * state
    return prefix + jnp.exp(-rates * (positions * x).astype(jnp.float32)) * above


def shards(tokens, input_weight, short_taps, residue, decay_rate, out_weight):
    f32, bf16 = jnp.float32, jnp.bfloat16
    rows, depth = tokens.shape
    width = input_weight.shape[2] // 2
    groups = lax.axis_size("chan")
    sides = lax.axis_size("y"), lax.axis_size("x")
    chips = sides[0] * sides[1]
    core, z = lax.axis_index("core"), lax.axis_index("chan")
    positions = 2 * rows
    sequence = positions * chips
    place = jnp.stack([z, core, lax.axis_index("y"), lax.axis_index("x")]).astype(jnp.int32)

    def own_columns(array, owner):
        return lax.dynamic_slice_in_dim(array, owner * width, width, axis=array.ndim - 1)

    def by_core(own, other, axis):
        return jnp.where(
            core == 0,
            jnp.concatenate([own, other], axis=axis),
            jnp.concatenate([other, own], axis=axis),
        )

    kept = own_columns(input_weight, core)
    got = swap_cores(own_columns(input_weight, 1 - core))
    both = by_core(kept, got, 1)
    query_weight = lax.all_gather(both[0], ("y", "x"), axis=0, tiled=True)
    weights = weights_around(jnp.concatenate([both[1], both[2]], axis=1), sides)

    other = swap_cores(tokens)
    low = jnp.where(core == 0, tokens, other)
    high = jnp.where(core == 0, other, tokens)
    earlier = lax.ppermute(
        high[-HALO:], ("y", "x", "core"), [(i, i + 2) for i in range(2 * chips - 2)]
    )
    gathered = []
    for stream in (low, jnp.concatenate([high, earlier], axis=0)):
        mine = tokens_around(stream, core)
        gathered += [stream, *mine, *[swap_cores(block) for block in mine]]

    rates_all = decay_rate / float(sequence)
    rates = own_columns(rates_all, core)
    amplitude = own_columns(residue * jnp.sqrt(-jnp.expm1(-2.0 * rates_all)), core)
    taps = own_columns(short_taps, core)
    modes = rates.shape[0]
    blocks = 8
    lanes = (width // 128, positions, 128)
    features = depth * groups
    dma = pltpu.SemaphoreType.DMA

    signal, block_ends, end_state = on_device(
        functools.partial(key_value_kernel, groups, sides),
        (
            jax.ShapeDtypeStruct(lanes, f32),
            jax.ShapeDtypeStruct((modes, blocks, width), f32),
            jax.ShapeDtypeStruct((modes, width), f32),
        ),
        [
            pltpu.VMEM((positions + HALO, features), bf16),
            pltpu.VMEM((features, 2 * width), bf16),
            pltpu.VMEM((positions + HALO, 2 * width), f32),
            dma((16,)),
            dma((18,)),
        ],
        4 * positions * features * width,
        23,
        place, *gathered, *weights, taps, rates,
    )
    start_state = carried_in(end_state, rates, positions)
    query = on_device(
        functools.partial(query_kernel, groups),
        jax.ShapeDtypeStruct((positions, width), f32),
        [
            pltpu.VMEM((positions + HALO, features), bf16),
            pltpu.VMEM((positions + HALO, width), f32),
            dma((18,)),
        ],
        2 * positions * features * width,
        18,
        place, *gathered, query_weight, taps,
    )
    gated = on_device(
        scan_kernel,
        jax.ShapeDtypeStruct((positions, width), bf16),
        [pltpu.VMEM((modes, blocks, width), f32), pltpu.VMEM(lanes, f32)],
        4 * modes * positions * width,
        0,
        signal, query, block_ends, start_state, rates, amplitude,
    )
    gated = by_core(gated, swap_cores(gated), 1)
    return reduced(gated, out_weight, core, z, groups)


def reduced(gated, out_weight, core, z, groups):
    rows = gated.shape[0] // 2
    width = out_weight.shape[1] // groups
    ahead = 1 - 2 * core

    def product(values, distance, first=0, columns=width):
        start = (z + ahead * distance) % groups * width + first
        weight = lax.dynamic_slice_in_dim(out_weight, start, columns, axis=1)
        return jnp.dot(values, weight, preferred_element_type=jnp.float32).astype(jnp.bfloat16)

    half = width // 2
    part = product(gated, 4, core * half, half)
    streams = [part[:rows], part[rows:]]
    for distance in (3, 2, 1):
        part = product(gated, distance)
        for number in range(2):
            arrived = group_ring(streams[number])
            if distance == 3:
                nothing = jnp.zeros_like(arrived)
                arrived = jnp.where(
                    core == 0,
                    jnp.concatenate([arrived, nothing], axis=1),
                    jnp.concatenate([nothing, arrived], axis=1),
                )
            streams[number] = part[number * rows : (number + 1) * rows] + arrived
    low, high = [group_ring(stream) for stream in streams]
    kept = jnp.where(core == 0, low, high)
    got = swap_cores(jnp.where(core == 0, high, low))
    own = product(lax.dynamic_slice_in_dim(gated, core * rows, rows, axis=0), 0)
    total = own.astype(jnp.float32) + kept.astype(jnp.float32) + got.astype(jnp.float32)
    return total.astype(jnp.bfloat16)


def solution(mesh):
    devices = mesh.devices.reshape(4, 4, 2, 8)
    chips = Mesh(devices, ("y", "x", "core", "chan"))
    seq = ("y", "x", "core")
    placed = (
        P(seq, "chan"),
        P(None, seq, "chan"),
        P(None, None, "chan"),
        P(None, "chan"),
        P(None, "chan"),
        P("chan", None),
    )
    return jax.shard_map(
        shards, mesh=chips, in_specs=placed, out_specs=P(seq, "chan"), check_vma=False
    )
```

```python
import functools

import jax
import jax.numpy as jnp
from jax import lax
from jax.experimental import pallas as pl
from jax.experimental.pallas import tpu as pltpu
from jax.sharding import Mesh, PartitionSpec as P

HALO = 16


def swap_cores(block):
    return lax.ppermute(block, "core", [(0, 1), (1, 0)])


def chip_ring(block, sides, stage, sign):
    ny, nx = sides
    pairs = []
    for y in range(ny):
        for x in range(nx):
            for c in range(2):
                to = (y, (x + sign) % nx) if c == stage else ((y + sign) % ny, x)
                pairs.append(((y * nx + x) * 2 + c, (to[0] * nx + to[1]) * 2 + c))
    return lax.ppermute(block, ("y", "x", "core"), pairs)


def group_ring(block):
    n = lax.axis_size("chan")
    pairs = []
    for c in range(2):
        for z in range(n):
            pairs.append((c * n + z, c * n + (z + 1 - 2 * c) % n))
    return lax.ppermute(block, ("core", "chan"), pairs)


def weights_around(block, sides):
    def ring(own, stage):
        half = own.shape[0] // 2
        before = chip_ring(own, sides, stage, 1)
        behind = chip_ring(own, sides, stage, -1)
        far = chip_ring(before[:half], sides, stage, 1), chip_ring(behind[half:], sides, stage, -1)
        return before, behind, far

    before, behind, far = ring(block, 0)
    near = jnp.concatenate([block, before, *far, behind], axis=0)
    before, behind, far = ring(near, 1)
    return near, before, behind, *far


def tokens_around(block, core):
    blocks = [block]
    for _ in range(3):
        blocks.append(group_ring(blocks[-1]))
    half = block.shape[1] // 2
    blocks.append(group_ring(lax.dynamic_slice_in_dim(blocks[-1], core * half, half, axis=1)))
    return blocks[1:]


def tokens_in_order(place, groups, blocks, gathered, semaphores):
    copies = []
    core = place[1]
    ahead = 1 - 2 * core
    own, mine, partner = blocks
    depth = own.shape[1]
    pieces = [(own, 0, 0, 0)]
    for distance, block in enumerate(mine, 1):
        pieces.append((block, -distance, distance == len(mine), core))
    for distance, block in enumerate(partner, 1):
        pieces.append((block, distance, distance == len(partner), 1 - core))
    for block, offset, halved, side in pieces:
        group = lax.rem(place[0] + offset * ahead + groups, groups)
        column = group * depth
        if halved:
            column = column + side * (depth // 2)
        column = pl.multiple_of(column, 128)
        copies.append(
            pltpu.make_async_copy(
                block,
                gathered.at[:, pl.ds(column, block.shape[1])],
                semaphores.at[len(copies)],
            )
        )
    for copy in copies:
        copy.start()
    return copies


def weights_in_order(place, sides, blocks, gathered, semaphores):
    ny, nx = sides
    core, y, x = place[1], place[2], place[3]
    near, before, behind, far_top, far_bottom = blocks
    rows = near.shape[0] // 4
    order = (0, -1, -2, 1)
    pieces = [(near, i, first, 0) for i, first in enumerate(order)]
    pieces += [(before, i, first, -1) for i, first in enumerate(order)]
    pieces += [(behind, i, first, 1) for i, first in enumerate(order)]
    pieces += [(far_top, i, order[i], -2) for i in range(2)]
    pieces += [(far_bottom, i, order[i + 2], -2) for i in range(2)]
    copies = []
    for block, i, first, second in pieces:
        dx = jnp.where(core == 0, first, second)
        dy = jnp.where(core == 0, second, first)
        chip = lax.rem(y + dy + ny, ny) * nx + lax.rem(x + dx + nx, nx)
        to = pl.multiple_of(chip * rows, 128)
        copies.append(
            pltpu.make_async_copy(
                block.at[pl.ds(i * rows, rows)],
                gathered.at[pl.ds(to, rows)],
                semaphores.at[len(copies)],
            )
        )
    for copy in copies:
        copy.start()
    return copies


def take_tokens(refs):
    return refs[0], refs[1:5], refs[5:9]


def project(tokens, weight, columns, projected):
    rows = tokens.shape[0] - HALO
    total = jnp.dot(tokens[...], weight[:, columns], preferred_element_type=jnp.float32)
    total = total.astype(jnp.bfloat16).astype(jnp.float32)
    projected[pl.ds(0, HALO), columns] = total[rows:]
    projected[pl.ds(HALO, rows), columns] = total[:rows]


def filtered(projected, taps, group, channels, columns):
    rows = projected.shape[0] - HALO
    return sum(
        taps[group, lag : lag + 1, channels] * projected[pl.ds(HALO - lag, rows), columns]
        for lag in range(taps.shape[1])
    )


def project_kernel(groups, sides, place, *refs):
    blocks, weights, query_weight = take_tokens(refs[:9]), refs[9:14], refs[14]
    taps, rates, query, signal, block_ends, end_state, tokens, weight, projected, *semaphores = refs[15:]
    width = query.shape[1]
    early = tokens_in_order(place, groups, blocks, tokens, semaphores[0])
    copy = pltpu.make_async_copy(
        query_weight, weight.at[:, pl.ds(2 * width, width)], semaphores[1].at[0]
    )
    copy.start()
    late = weights_in_order(place, sides, weights, weight.at[:, pl.ds(0, 2 * width)], semaphores[2])
    for each in early + [copy]:
        each.wait()
    project(tokens, weight, pl.ds(2 * width, width), projected)
    query[...] = filtered(projected, taps, 0, slice(None), pl.ds(2 * width, width))
    for each in late:
        each.wait()
    project(tokens, weight, pl.ds(0, 2 * width), projected)
    modes, blocks, width = block_ends.shape
    steps = signal.shape[1] // blocks
    for part in range(width // 128):
        lanes = pl.ds(part * 128, 128)
        key = filtered(projected, taps, 1, lanes, lanes)
        value = filtered(projected, taps, 2, lanes, pl.ds(width + part * 128, 128))
        signal[part] = key * value
        decay = [
            jnp.broadcast_to(jnp.exp(-rates[m : m + 1, lanes]), (blocks, 128)) for m in range(modes)
        ]

        def step(s, states):
            u = signal[part, pl.ds(s, blocks, steps), :]
            return tuple(decay[m] * states[m] + u for m in range(modes))

        zero = jnp.zeros((blocks, 128), jnp.float32)
        states = lax.fori_loop(0, steps, step, (zero,) * modes, unroll=8)
        for m in range(modes):
            block_ends[m, :, lanes] = states[m]
    block_decay = jnp.exp(-rates[...] * float(steps))
    state = block_ends[:, 0, :]
    for b in range(1, blocks):
        state = block_decay * state + block_ends[:, b, :]
    end_state[...] = state


def scan_kernel(place, signal, query, block_ends, states, rates, amplitude, gated, block_starts, result):
    modes, blocks, width = block_ends.shape
    steps = signal.shape[1] // blocks
    chip_decay = jnp.exp(-rates[...] * float(steps * blocks))
    state = jnp.zeros((modes, width), jnp.float32)
    for chip in range(states.shape[0] - 1):
        state = jnp.where(chip < place[4], chip_decay * state + states[chip], state)
    block_decay = jnp.exp(-rates[...] * float(steps))
    for b in range(blocks):
        block_starts[:, b, :] = state
        state = block_decay * state + block_ends[:, b, :]
    for part in range(width // 128):
        lanes = pl.ds(part * 128, 128)
        decay = [
            jnp.broadcast_to(jnp.exp(-rates[m : m + 1, lanes]), (blocks, 128)) for m in range(modes)
        ]
        scale = [jnp.broadcast_to(amplitude[m : m + 1, lanes], (blocks, 128)) for m in range(modes)]

        def step(s, states):
            u = signal[part, pl.ds(s, blocks, steps), :]
            states = tuple(decay[m] * states[m] + u for m in range(modes))
            terms = [scale[m] * states[m] for m in range(modes)]
            while len(terms) > 1:
                terms = [a + b for a, b in zip(terms[::2], terms[1::2])]
            result[part, pl.ds(s, blocks, steps), :] = terms[0]
            return states

        states_now = tuple(block_starts[m, :, lanes] for m in range(modes))
        lax.fori_loop(0, steps, step, states_now, unroll=4)
        gated[:, lanes] = (query[:, lanes] * result[part]).astype(jnp.bfloat16)


def on_device(kernel, outs, scratch, cost, limit, copied, place, *arrays):
    smem = pl.BlockSpec(memory_space=pltpu.SMEM)
    vmem = pl.BlockSpec(memory_space=pltpu.VMEM)
    hbm = pl.BlockSpec(memory_space=pltpu.HBM)
    kept = [pltpu.with_memory_space_constraint(a, pltpu.HBM) for a in arrays[:copied]]
    return pl.pallas_call(
        kernel,
        out_shape=outs,
        in_specs=[smem] + [hbm] * copied + [vmem] * (len(arrays) - copied),
        out_specs=jax.tree.map(lambda _: vmem, outs),
        scratch_shapes=scratch,
        compiler_params=pltpu.CompilerParams(vmem_limit_bytes=limit * 1024 * 1024),
        cost_estimate=pl.CostEstimate(flops=cost, bytes_accessed=cost // 400, transcendentals=0),
    )(place, *kept, *arrays[copied:])


def shards(tokens, input_weight, short_taps, residue, decay_rate, out_weight):
    f32, bf16 = jnp.float32, jnp.bfloat16
    rows, depth = tokens.shape
    width = input_weight.shape[2] // 2
    groups = lax.axis_size("chan")
    sides = lax.axis_size("y"), lax.axis_size("x")
    chips = sides[0] * sides[1]
    core, z = lax.axis_index("core"), lax.axis_index("chan")
    positions = 2 * rows
    sequence = positions * chips
    y, x = lax.axis_index("y"), lax.axis_index("x")
    place = jnp.stack([z, core, y, x, y * sides[1] + x]).astype(jnp.int32)

    def own_columns(array, owner):
        return lax.dynamic_slice_in_dim(array, owner * width, width, axis=array.ndim - 1)

    def by_core(own, other, axis):
        return jnp.where(
            core == 0,
            jnp.concatenate([own, other], axis=axis),
            jnp.concatenate([other, own], axis=axis),
        )

    other = swap_cores(tokens)
    block = by_core(tokens, other, 0)
    earlier = lax.ppermute(
        block[-HALO:], ("y", "x", "core"), [(i, i + 2) for i in range(2 * chips - 2)]
    )
    block = jnp.concatenate([block, earlier], axis=0)
    mine = tokens_around(block, core)
    gathered = [block, *mine, *[swap_cores(each) for each in mine]]

    kept = own_columns(input_weight, core)
    got = swap_cores(own_columns(input_weight, 1 - core))
    both = by_core(kept, got, 1)
    query_weight = lax.all_gather(both[0].reshape(-1, width), ("y", "x"), axis=0, tiled=True)
    key_value, _ = lax.optimization_barrier((jnp.concatenate([both[1], both[2]], axis=1), other))
    weights = weights_around(key_value, sides)

    rates_all = decay_rate / float(sequence)
    rates = own_columns(rates_all, core)
    amplitude = own_columns(residue * jnp.sqrt(-jnp.expm1(-2.0 * rates_all)), core)
    taps = own_columns(short_taps, core)
    modes = rates.shape[0]
    blocks = 8
    lanes = (width // 128, positions, 128)
    features = depth * groups
    dma = pltpu.SemaphoreType.DMA

    query, signal, block_ends, end_state = on_device(
        functools.partial(project_kernel, groups, sides),
        (
            jax.ShapeDtypeStruct((positions, width), f32),
            jax.ShapeDtypeStruct(lanes, f32),
            jax.ShapeDtypeStruct((modes, blocks, width), f32),
            jax.ShapeDtypeStruct((modes, width), f32),
        ),
        [
            pltpu.VMEM((positions + HALO, features), bf16),
            pltpu.VMEM((features, 3 * width), bf16),
            pltpu.VMEM((positions + HALO, 3 * width), f32),
            dma((9,)),
            dma((1,)),
            dma((16,)),
        ],
        6 * positions * features * width,
        24,
        15,
        place, *gathered, *weights, query_weight, taps, rates,
    )
    states = lax.all_to_all(
        jnp.broadcast_to(end_state[None], (chips, modes, width)), ("y", "x"), 0, 0, tiled=True
    )
    gated = on_device(
        scan_kernel,
        jax.ShapeDtypeStruct((positions, width), bf16),
        [pltpu.VMEM((modes, blocks, width), f32), pltpu.VMEM(lanes, f32)],
        4 * modes * positions * width,
        12,
        0,
        place, signal, query, block_ends, states, rates, amplitude,
    )
    gated = by_core(gated, swap_cores(gated), 1)
    return reduced(gated, out_weight, core, z, groups)


def reduced(gated, out_weight, core, z, groups):
    rows = gated.shape[0] // 2
    width = out_weight.shape[1] // groups
    ahead = 1 - 2 * core

    def product(values, distance, first=0, columns=width):
        start = (z + ahead * distance) % groups * width + first
        weight = lax.dynamic_slice_in_dim(out_weight, start, columns, axis=1)
        return jnp.dot(values, weight, preferred_element_type=jnp.float32).astype(jnp.bfloat16)

    half = width // 2
    part = product(gated, 4, core * half, half)
    cut = rows - 16
    spans = slice(0, cut), slice(cut, 2 * rows)
    streams = [part[span] for span in spans]
    own = product(lax.dynamic_slice_in_dim(gated, core * rows, rows, axis=0), 0)
    for distance in (3, 2, 1):
        part = product(gated, distance)
        for number, span in enumerate(spans):
            arrived = group_ring(streams[number])
            if distance == 3:
                nothing = jnp.zeros_like(arrived)
                arrived = jnp.where(
                    core == 0,
                    jnp.concatenate([arrived, nothing], axis=1),
                    jnp.concatenate([nothing, arrived], axis=1),
                )
            before = own if number == 0 else streams[0]
            arrived, _ = lax.optimization_barrier((arrived, before))
            streams[number] = part[span] + arrived
    total = jnp.concatenate([group_ring(stream) for stream in streams], axis=0)
    kept = lax.dynamic_slice_in_dim(total, core * rows, rows, axis=0)
    got = swap_cores(lax.dynamic_slice_in_dim(total, (1 - core) * rows, rows, axis=0))
    total = own.astype(jnp.float32) + kept.astype(jnp.float32) + got.astype(jnp.float32)
    return total.astype(jnp.bfloat16)


def solution(mesh):
    devices = mesh.devices.reshape(4, 4, 2, 8)
    chips = Mesh(devices, ("y", "x", "core", "chan"))
    seq = ("y", "x", "core")
    placed = (
        P(seq, "chan"),
        P(None, seq, "chan"),
        P(None, None, "chan"),
        P(None, "chan"),
        P(None, "chan"),
        P("chan", None),
    )
    return jax.shard_map(
        shards, mesh=chips, in_specs=placed, out_specs=P(seq, "chan"), check_vma=False
    )
```

```python
import functools

import jax
import jax.numpy as jnp
from jax import lax
from jax.experimental import pallas as pl
from jax.experimental.pallas import tpu as pltpu
from jax.sharding import Mesh, PartitionSpec as P

HALO = 16


def swap_cores(block):
    return lax.ppermute(block, "core", [(0, 1), (1, 0)])


def chip_ring(block, sides, stage, sign):
    ny, nx = sides
    pairs = []
    for y in range(ny):
        for x in range(nx):
            for c in range(2):
                to = (y, (x + sign) % nx) if c == stage else ((y + sign) % ny, x)
                pairs.append(((y * nx + x) * 2 + c, (to[0] * nx + to[1]) * 2 + c))
    return lax.ppermute(block, ("y", "x", "core"), pairs)


def group_ring(block):
    n = lax.axis_size("chan")
    pairs = []
    for c in range(2):
        for z in range(n):
            pairs.append((c * n + z, c * n + (z + 1 - 2 * c) % n))
    return lax.ppermute(block, ("core", "chan"), pairs)


def ring(own, sides, stage):
    return chip_ring(own, sides, stage, 1), chip_ring(own, sides, stage, -1)


def far_side(before, behind, sides, stage):
    half = before.shape[0] // 2
    return chip_ring(before[:half], sides, stage, 1), chip_ring(behind[half:], sides, stage, -1)


def tokens_in_order(place, groups, blocks, gathered, semaphores):
    copies = []
    core = place[1]
    ahead = 1 - 2 * core
    own, mine, partner = blocks
    depth = own.shape[1]
    pieces = [(own, 0, 0, 0)]
    for distance, block in enumerate(mine, 1):
        pieces.append((block, -distance, distance == len(mine), core))
    for distance, block in enumerate(partner, 1):
        pieces.append((block, distance, distance == len(partner), 1 - core))
    for block, offset, halved, side in pieces:
        group = lax.rem(place[0] + offset * ahead + groups, groups)
        column = group * depth
        if halved:
            column = column + side * (depth // 2)
        column = pl.multiple_of(column, 128)
        copies.append(
            pltpu.make_async_copy(
                block,
                gathered.at[:, pl.ds(column, block.shape[1])],
                semaphores.at[len(copies)],
            )
        )
    for copy in copies:
        copy.start()
    return copies


def weights_in_order(place, sides, blocks, gathered, semaphores):
    ny, nx = sides
    core, y, x = place[1], place[2], place[3]
    near, before, behind, *far = blocks
    rows = near.shape[0] // 4
    order = (0, -1, -2, 1)
    pieces = []
    for block, second in ((near, 0), (before, -1), (behind, 1)):
        pieces += [(block, i, first, second) for i, first in enumerate(order)]
    if len(far) == 1:
        pieces += [(far[0], i, first, -2) for i, first in enumerate(order)]
    else:
        pieces += [(far[i // 2], i % 2, first, -2) for i, first in enumerate(order)]
    copies = []
    for block, i, first, second in pieces:
        dx = jnp.where(core == 0, first, second)
        dy = jnp.where(core == 0, second, first)
        chip = lax.rem(y + dy + ny, ny) * nx + lax.rem(x + dx + nx, nx)
        to = pl.multiple_of(chip * rows, 128)
        copies.append(
            pltpu.make_async_copy(
                block.at[pl.ds(i * rows, rows)],
                gathered.at[pl.ds(to, rows)],
                semaphores.at[len(copies)],
            )
        )
    for copy in copies:
        copy.start()
    return copies


def near_kernel(own, before, far_top, far_bottom, behind, key_value, query):
    split = key_value.shape[1]
    row = 0
    for block in (own, before, far_top, far_bottom, behind):
        rows = block.shape[0]
        key_value[pl.ds(row, rows), :] = block[:, pl.ds(0, split)]
        query[pl.ds(row, rows), :] = block[:, pl.ds(split, query.shape[1])]
        row += rows


def take_tokens(refs):
    return refs[0], refs[1:5], refs[5:9]


def project(tokens, weight, projected):
    rows = tokens.shape[0] - HALO
    total = jnp.dot(tokens[...], weight[...], preferred_element_type=jnp.float32)
    total = total.astype(jnp.bfloat16).astype(jnp.float32)
    projected[pl.ds(0, HALO), :] = total[rows:]
    projected[pl.ds(HALO, rows), :] = total[:rows]


def filtered(projected, taps, group, channels, columns):
    rows = projected.shape[0] - HALO
    return sum(
        taps[group, lag : lag + 1, channels] * projected[pl.ds(HALO - lag, rows), columns]
        for lag in range(taps.shape[1])
    )


def query_kernel(groups, sides, place, *refs):
    blocks, weights = take_tokens(refs[:9]), refs[9:13]
    taps, query, tokens, weight, projected, *semaphores = refs[13:]
    copies = tokens_in_order(place, groups, blocks, tokens, semaphores[0])
    copies += weights_in_order(place, sides, weights, weight, semaphores[1])
    for copy in copies:
        copy.wait()
    project(tokens, weight, projected)
    query[...] = filtered(projected, taps, 0, slice(None), slice(None))


def key_value_kernel(groups, sides, place, *refs):
    blocks, weights = take_tokens(refs[:9]), refs[9:14]
    taps, rates, signal, block_ends, end_state, tokens, weight, projected, *semaphores = refs[14:]
    copies = tokens_in_order(place, groups, blocks, tokens, semaphores[0])
    copies += weights_in_order(place, sides, weights, weight, semaphores[1])
    for copy in copies:
        copy.wait()
    project(tokens, weight, projected)
    modes, blocks, width = block_ends.shape
    steps = signal.shape[1] // blocks
    for part in range(width // 128):
        lanes = pl.ds(part * 128, 128)
        key = filtered(projected, taps, 1, lanes, lanes)
        value = filtered(projected, taps, 2, lanes, pl.ds(width + part * 128, 128))
        signal[part] = key * value
        decay = [
            jnp.broadcast_to(jnp.exp(-rates[m : m + 1, lanes]), (blocks, 128)) for m in range(modes)
        ]

        def step(s, states):
            u = signal[part, pl.ds(s, blocks, steps), :]
            return tuple(decay[m] * states[m] + u for m in range(modes))

        zero = jnp.zeros((blocks, 128), jnp.float32)
        states = lax.fori_loop(0, steps, step, (zero,) * modes, unroll=8)
        for m in range(modes):
            block_ends[m, :, lanes] = states[m]
    block_decay = jnp.exp(-rates[...] * float(steps))
    state = block_ends[:, 0, :]
    for b in range(1, blocks):
        state = block_decay * state + block_ends[:, b, :]
    for chip in range(end_state.shape[0]):
        end_state[chip] = state


def scan_kernel(place, signal, query, block_ends, states, rates, amplitude, gated, block_starts, result):
    modes, blocks, width = block_ends.shape
    steps = signal.shape[1] // blocks
    chip_decay = jnp.exp(-rates[...] * float(steps * blocks))
    state = jnp.zeros((modes, width), jnp.float32)
    for chip in range(states.shape[0] - 1):
        state = jnp.where(chip < place[4], chip_decay * state + states[chip], state)
    block_decay = jnp.exp(-rates[...] * float(steps))
    for b in range(blocks):
        block_starts[:, b, :] = state
        state = block_decay * state + block_ends[:, b, :]
    for part in range(width // 128):
        lanes = pl.ds(part * 128, 128)
        decay = [
            jnp.broadcast_to(jnp.exp(-rates[m : m + 1, lanes]), (blocks, 128)) for m in range(modes)
        ]
        scale = [jnp.broadcast_to(amplitude[m : m + 1, lanes], (blocks, 128)) for m in range(modes)]

        def step(s, states):
            u = signal[part, pl.ds(s, blocks, steps), :]
            states = tuple(decay[m] * states[m] + u for m in range(modes))
            terms = [scale[m] * states[m] for m in range(modes)]
            while len(terms) > 1:
                terms = [a + b for a, b in zip(terms[::2], terms[1::2])]
            result[part, pl.ds(s, blocks, steps), :] = terms[0]
            return states

        states_now = tuple(block_starts[m, :, lanes] for m in range(modes))
        lax.fori_loop(0, steps, step, states_now, unroll=4)
        gated[:, lanes] = (query[:, lanes] * result[part]).astype(jnp.bfloat16)


def on_device(kernel, outs, scratch, cost, limit, copied, place, *arrays):
    smem = pl.BlockSpec(memory_space=pltpu.SMEM)
    vmem = pl.BlockSpec(memory_space=pltpu.VMEM)
    hbm = pl.BlockSpec(memory_space=pltpu.HBM)
    kept = [pltpu.with_memory_space_constraint(a, pltpu.HBM) for a in arrays[:copied]]
    return pl.pallas_call(
        kernel,
        out_shape=outs,
        in_specs=[smem] + [hbm] * copied + [vmem] * (len(arrays) - copied),
        out_specs=jax.tree.map(lambda _: vmem, outs),
        scratch_shapes=scratch,
        compiler_params=pltpu.CompilerParams(vmem_limit_bytes=limit * 1024 * 1024),
        cost_estimate=pl.CostEstimate(flops=cost, bytes_accessed=cost // 400, transcendentals=0),
    )(place, *kept, *arrays[copied:])


def shards(tokens, input_weight, short_taps, residue, decay_rate, out_weight):
    f32, bf16 = jnp.float32, jnp.bfloat16
    rows, depth = tokens.shape
    width = input_weight.shape[2] // 2
    groups = lax.axis_size("chan")
    sides = lax.axis_size("y"), lax.axis_size("x")
    chips = sides[0] * sides[1]
    core, z = lax.axis_index("core"), lax.axis_index("chan")
    positions = 2 * rows
    sequence = positions * chips
    y, x = lax.axis_index("y"), lax.axis_index("x")
    place = jnp.stack([z, core, y, x, y * sides[1] + x]).astype(jnp.int32)

    def own_columns(array, owner):
        return lax.dynamic_slice_in_dim(array, owner * width, width, axis=array.ndim - 1)

    def by_core(own, other, axis):
        return jnp.where(
            core == 0,
            jnp.concatenate([own, other], axis=axis),
            jnp.concatenate([other, own], axis=axis),
        )

    other = swap_cores(tokens)
    block = by_core(tokens, other, 0)
    earlier = lax.ppermute(
        block[-HALO:], ("y", "x", "core"), [(i, i + 2) for i in range(2 * chips - 2)]
    )
    block = jnp.concatenate([block, earlier], axis=0)
    kept = own_columns(input_weight, core)
    given, _ = lax.optimization_barrier((own_columns(input_weight, 1 - core), other))
    both = by_core(kept, swap_cores(given), 1)
    own = jnp.concatenate([both[1], both[2], both[0]], axis=1)
    before, behind = first_ring = ring(own, sides, 0)
    vmem = pl.BlockSpec(memory_space=pltpu.VMEM)
    near, near_query = pl.pallas_call(
        near_kernel,
        out_shape=(
            jax.ShapeDtypeStruct((4 * own.shape[0], 2 * width), bf16),
            jax.ShapeDtypeStruct((4 * own.shape[0], width), bf16),
        ),
        in_specs=[vmem] * 5,
        out_specs=(vmem, vmem),
        compiler_params=pltpu.CompilerParams(vmem_limit_bytes=8 * 1024 * 1024),
        cost_estimate=pl.CostEstimate(flops=0, bytes_accessed=8 * own.size * 2, transcendentals=0),
    )(own, before, *far_side(before, behind, sides, 0), behind)
    before, behind = ring(near, sides, 1)

    mine = [group_ring(block)]
    second, *_ = lax.optimization_barrier((mine[0], *first_ring))
    mine.append(group_ring(second))
    mine.append(group_ring(mine[1]))
    last = lax.dynamic_slice_in_dim(mine[-1], core * (depth // 2), depth // 2, axis=1)
    shared = [swap_cores(each) for each in mine[:2]]
    last, *shared = lax.optimization_barrier((last, *shared))
    mine.append(group_ring(last))
    far = far_side(before, behind, sides, 1)
    query_ring = ring(near_query, sides, 1)
    *rest, top, bottom, before_query, behind_query = lax.optimization_barrier(
        (*mine[2:], *far, *query_ring)
    )
    weights = near, before, behind, top, bottom
    query_weights = near_query, before_query, behind_query, chip_ring(near_query, sides, 1, 2)
    gathered = [block, *mine, *shared, *[swap_cores(each) for each in rest]]

    rates_all = decay_rate / float(sequence)
    rates = own_columns(rates_all, core)
    amplitude = own_columns(residue * jnp.sqrt(-jnp.expm1(-2.0 * rates_all)), core)
    taps = own_columns(short_taps, core)
    modes = rates.shape[0]
    blocks = 8
    lanes = (width // 128, positions, 128)
    features = depth * groups
    dma = pltpu.SemaphoreType.DMA

    signal, block_ends, end_state = on_device(
        functools.partial(key_value_kernel, groups, sides),
        (
            jax.ShapeDtypeStruct(lanes, f32),
            jax.ShapeDtypeStruct((modes, blocks, width), f32),
            jax.ShapeDtypeStruct((chips, modes, width), f32),
        ),
        [
            pltpu.VMEM((positions + HALO, features), bf16),
            pltpu.VMEM((features, 2 * width), bf16),
            pltpu.VMEM((positions + HALO, 2 * width), f32),
            dma((9,)),
            dma((16,)),
        ],
        4 * positions * features * width,
        20,
        14,
        place, *gathered, *weights, taps, rates,
    )
    states = lax.all_to_all(end_state, ("y", "x"), 0, 0, tiled=True)
    query = on_device(
        functools.partial(query_kernel, groups, sides),
        jax.ShapeDtypeStruct((positions, width), f32),
        [
            pltpu.VMEM((positions + HALO, features), bf16),
            pltpu.VMEM((features, width), bf16),
            pltpu.VMEM((positions + HALO, width), f32),
            dma((9,)),
            dma((16,)),
        ],
        2 * positions * features * width,
        16,
        13,
        place, *gathered, *query_weights, taps,
    )
    gated = on_device(
        scan_kernel,
        jax.ShapeDtypeStruct((positions, width), bf16),
        [pltpu.VMEM((modes, blocks, width), f32), pltpu.VMEM(lanes, f32)],
        4 * modes * positions * width,
        12,
        0,
        place, signal, query, block_ends, states, rates, amplitude,
    )
    given = swap_cores(lax.dynamic_slice_in_dim(gated, (1 - core) * rows, rows, axis=0))
    gated = by_core(lax.dynamic_slice_in_dim(gated, core * rows, rows, axis=0), given, 1)
    return reduced(gated, out_weight, z, groups)


def reduced(gated, out_weight, z, groups):
    width = out_weight.shape[1] // groups

    def send(block, direction):
        return lax.ppermute(block, "chan", [(i, (i + direction) % groups) for i in range(groups)])

    def product(distance):
        start = (z + distance) % groups * width
        weight = lax.dynamic_slice_in_dim(out_weight, start, width, axis=1)
        total = jnp.dot(gated, weight, preferred_element_type=jnp.float32).astype(jnp.bfloat16)
        return lax.optimization_barrier(total)

    half = width // 2
    part = product(4)
    ahead, behind = part[:, :half], part[:, half:]
    own = product(0)
    for distance in (3, 2, 1):
        ahead_part, behind_part = product(distance), product(-distance)
        ahead, behind = send(ahead, 1), send(behind, -1)
        if distance == 3:
            ahead = jnp.concatenate([ahead, jnp.zeros_like(ahead)], axis=1)
            behind = jnp.concatenate([jnp.zeros_like(behind), behind], axis=1)
        ahead = ahead_part + ahead
        behind, _ = lax.optimization_barrier((behind, ahead))
        behind = behind_part + behind
    ahead, behind = send(ahead, 1), send(behind, -1)
    total = own.astype(jnp.float32) + ahead.astype(jnp.float32) + behind.astype(jnp.float32)
    return total.astype(jnp.bfloat16)


def solution(mesh):
    devices = mesh.devices.reshape(4, 4, 2, 8)
    chips = Mesh(devices, ("y", "x", "core", "chan"))
    seq = ("y", "x", "core")
    placed = (
        P(seq, "chan"),
        P(None, seq, "chan"),
        P(None, None, "chan"),
        P(None, "chan"),
        P(None, "chan"),
        P("chan", None),
    )
    return jax.shard_map(
        shards, mesh=chips, in_specs=placed, out_specs=P(seq, "chan"), check_vma=False
    )
```

```python
import functools

import jax
import jax.numpy as jnp
from jax import lax
from jax.experimental import pallas as pl
from jax.experimental.pallas import tpu as pltpu
from jax.sharding import Mesh, PartitionSpec as P

HALO = 16


def swap_cores(block):
    return lax.ppermute(block, "core", [(0, 1), (1, 0)])


def chip_ring(block, sides, stage, sign):
    ny, nx = sides
    pairs = []
    for y in range(ny):
        for x in range(nx):
            for c in range(2):
                to = (y, (x + sign) % nx) if c == stage else ((y + sign) % ny, x)
                pairs.append(((y * nx + x) * 2 + c, (to[0] * nx + to[1]) * 2 + c))
    return lax.ppermute(block, ("y", "x", "core"), pairs)


def group_ring(block, hops=1):
    n = lax.axis_size("chan")
    pairs = []
    for c in range(2):
        for z in range(n):
            pairs.append((c * n + z, c * n + (z + (1 - 2 * c) * hops) % n))
    return lax.ppermute(block, ("core", "chan"), pairs)


def ring(own, sides, stage):
    return chip_ring(own, sides, stage, 1), chip_ring(own, sides, stage, -1)


def far_side(before, behind, sides, stage):
    half = before.shape[0] // 2
    return chip_ring(before[:half], sides, stage, 1), chip_ring(behind[half:], sides, stage, -1)


def tokens_in_order(place, groups, blocks, gathered, semaphores):
    copies = []
    core = place[1]
    ahead = 1 - 2 * core
    own, mine, partner = blocks
    depth = own.shape[1]
    pieces = [(own, 0, 0, 0)]
    for distance, block in enumerate(mine, 1):
        pieces.append((block, -distance, distance == len(mine), core))
    for distance, block in enumerate(partner, 1):
        pieces.append((block, distance, distance == len(partner), 1 - core))
    for block, offset, halved, side in pieces:
        group = lax.rem(place[0] + offset * ahead + groups, groups)
        column = group * depth
        if halved:
            column = column + side * (depth // 2)
        column = pl.multiple_of(column, 128)
        copies.append(
            pltpu.make_async_copy(
                block,
                gathered.at[:, pl.ds(column, block.shape[1])],
                semaphores.at[len(copies)],
            )
        )
    for copy in copies:
        copy.start()
    return copies


def weights_in_order(place, sides, blocks, gathered, semaphores):
    ny, nx = sides
    core, y, x = place[1], place[2], place[3]
    near, before, behind, *far = blocks
    rows = near.shape[0] // 4
    order = (0, -1, -2, 1)
    pieces = []
    for block, second in ((near, 0), (before, -1), (behind, 1)):
        pieces += [(block, i, first, second) for i, first in enumerate(order)]
    if len(far) == 1:
        pieces += [(far[0], i, first, -2) for i, first in enumerate(order)]
    else:
        pieces += [(far[i // 2], i % 2, first, -2) for i, first in enumerate(order)]
    copies = []
    for block, i, first, second in pieces:
        dx = jnp.where(core == 0, first, second)
        dy = jnp.where(core == 0, second, first)
        chip = lax.rem(y + dy + ny, ny) * nx + lax.rem(x + dx + nx, nx)
        to = pl.multiple_of(chip * rows, 128)
        copies.append(
            pltpu.make_async_copy(
                block.at[pl.ds(i * rows, rows)],
                gathered.at[pl.ds(to, rows)],
                semaphores.at[len(copies)],
            )
        )
    for copy in copies:
        copy.start()
    return copies


def near_kernel(own, before, far_top, far_bottom, behind, key_value, query):
    split = key_value.shape[1]
    row = 0
    for block in (own, before, far_top, far_bottom, behind):
        rows = block.shape[0]
        key_value[pl.ds(row, rows), :] = block[:, pl.ds(0, split)]
        query[pl.ds(row, rows), :] = block[:, pl.ds(split, query.shape[1])]
        row += rows


def take_tokens(refs):
    return refs[0], refs[1:5], refs[5:9]


def project(tokens, weight, projected):
    rows = tokens.shape[0] - HALO
    total = jnp.dot(tokens[...], weight[...], preferred_element_type=jnp.float32)
    total = total.astype(jnp.bfloat16).astype(jnp.float32)
    projected[pl.ds(0, HALO), :] = total[rows:]
    projected[pl.ds(HALO, rows), :] = total[:rows]


def filtered(projected, taps, group, channels, columns):
    rows = projected.shape[0] - HALO
    return sum(
        taps[group, lag : lag + 1, channels] * projected[pl.ds(HALO - lag, rows), columns]
        for lag in range(taps.shape[1])
    )


def query_kernel(groups, sides, place, *refs):
    blocks, weights = take_tokens(refs[:9]), refs[9:13]
    taps, query, tokens, weight, projected, *semaphores = refs[13:]
    copies = tokens_in_order(place, groups, blocks, tokens, semaphores[0])
    copies += weights_in_order(place, sides, weights, weight, semaphores[1])
    for copy in copies:
        copy.wait()
    project(tokens, weight, projected)
    query[...] = filtered(projected, taps, 0, slice(None), slice(None))


def key_value_kernel(groups, sides, place, *refs):
    blocks, weights = take_tokens(refs[:9]), refs[9:14]
    taps, rates, signal, block_ends, end_state, tokens, weight, projected, *semaphores = refs[14:]
    copies = tokens_in_order(place, groups, blocks, tokens, semaphores[0])
    copies += weights_in_order(place, sides, weights, weight, semaphores[1])
    for copy in copies:
        copy.wait()
    project(tokens, weight, projected)
    modes, blocks, width = block_ends.shape
    steps = signal.shape[1] // blocks
    for part in range(width // 128):
        lanes = pl.ds(part * 128, 128)
        key = filtered(projected, taps, 1, lanes, lanes)
        value = filtered(projected, taps, 2, lanes, pl.ds(width + part * 128, 128))
        signal[part] = key * value
        decay = [
            jnp.broadcast_to(jnp.exp(-rates[m : m + 1, lanes]), (blocks, 128)) for m in range(modes)
        ]

        def step(s, states):
            u = signal[part, pl.ds(s, blocks, steps), :]
            return tuple(decay[m] * states[m] + u for m in range(modes))

        zero = jnp.zeros((blocks, 128), jnp.float32)
        states = lax.fori_loop(0, steps, step, (zero,) * modes, unroll=8)
        for m in range(modes):
            block_ends[m, :, lanes] = states[m]
    block_decay = jnp.exp(-rates[...] * float(steps))
    state = block_ends[:, 0, :]
    for b in range(1, blocks):
        state = block_decay * state + block_ends[:, b, :]
    for chip in range(end_state.shape[0]):
        end_state[chip] = state


def scan_kernel(place, out_weight, signal, query, block_ends, states, rates, amplitude, *refs):
    gated, out_weight_near, block_starts, result, semaphore = refs
    copy = pltpu.make_async_copy(out_weight, out_weight_near, semaphore.at[0])
    copy.start()
    modes, blocks, width = block_ends.shape
    steps = signal.shape[1] // blocks
    chip_decay = jnp.exp(-rates[...] * float(steps * blocks))
    state = jnp.zeros((modes, width), jnp.float32)
    for chip in range(states.shape[0] - 1):
        state = jnp.where(chip < place[4], chip_decay * state + states[chip], state)
    block_decay = jnp.exp(-rates[...] * float(steps))
    for b in range(blocks):
        block_starts[:, b, :] = state
        state = block_decay * state + block_ends[:, b, :]
    for part in range(width // 128):
        lanes = pl.ds(part * 128, 128)
        decay = [
            jnp.broadcast_to(jnp.exp(-rates[m : m + 1, lanes]), (blocks, 128)) for m in range(modes)
        ]
        scale = [jnp.broadcast_to(amplitude[m : m + 1, lanes], (blocks, 128)) for m in range(modes)]

        def step(s, states):
            u = signal[part, pl.ds(s, blocks, steps), :]
            states = tuple(decay[m] * states[m] + u for m in range(modes))
            terms = [scale[m] * states[m] for m in range(modes)]
            while len(terms) > 1:
                terms = [a + b for a, b in zip(terms[::2], terms[1::2])]
            result[part, pl.ds(s, blocks, steps), :] = terms[0]
            return states

        states_now = tuple(block_starts[m, :, lanes] for m in range(modes))
        lax.fori_loop(0, steps, step, states_now, unroll=4)
        gated[:, lanes] = (query[:, lanes] * result[part]).astype(jnp.bfloat16)
    copy.wait()


def on_device(kernel, outs, scratch, cost, limit, copied, place, *arrays):
    smem = pl.BlockSpec(memory_space=pltpu.SMEM)
    vmem = pl.BlockSpec(memory_space=pltpu.VMEM)
    hbm = pl.BlockSpec(memory_space=pltpu.HBM)
    kept = [pltpu.with_memory_space_constraint(a, pltpu.HBM) for a in arrays[:copied]]
    return pl.pallas_call(
        kernel,
        out_shape=outs,
        in_specs=[smem] + [hbm] * copied + [vmem] * (len(arrays) - copied),
        out_specs=jax.tree.map(lambda _: vmem, outs),
        scratch_shapes=scratch,
        compiler_params=pltpu.CompilerParams(vmem_limit_bytes=limit * 1024 * 1024),
        cost_estimate=pl.CostEstimate(flops=cost, bytes_accessed=cost // 400, transcendentals=0),
    )(place, *kept, *arrays[copied:])


def shards(tokens, input_weight, short_taps, residue, decay_rate, out_weight):
    f32, bf16 = jnp.float32, jnp.bfloat16
    rows, depth = tokens.shape
    width = input_weight.shape[2] // 2
    groups = lax.axis_size("chan")
    sides = lax.axis_size("y"), lax.axis_size("x")
    chips = sides[0] * sides[1]
    core, z = lax.axis_index("core"), lax.axis_index("chan")
    positions = 2 * rows
    sequence = positions * chips
    y, x = lax.axis_index("y"), lax.axis_index("x")
    place = jnp.stack([z, core, y, x, y * sides[1] + x]).astype(jnp.int32)

    def own_columns(array, owner):
        return lax.dynamic_slice_in_dim(array, owner * width, width, axis=array.ndim - 1)

    def by_core(own, other, axis):
        return jnp.where(
            core == 0,
            jnp.concatenate([own, other], axis=axis),
            jnp.concatenate([other, own], axis=axis),
        )

    other = swap_cores(tokens)
    block = by_core(tokens, other, 0)
    earlier = lax.ppermute(
        block[-HALO:], ("y", "x", "core"), [(i, i + 2) for i in range(2 * chips - 2)]
    )
    block = jnp.concatenate([block, earlier], axis=0)
    kept = own_columns(input_weight, core)
    given, _ = lax.optimization_barrier((own_columns(input_weight, 1 - core), other))
    both = by_core(kept, swap_cores(given), 1)
    own = jnp.concatenate([both[1], both[2], both[0]], axis=1)
    before, behind = first_ring = ring(own, sides, 0)
    vmem = pl.BlockSpec(memory_space=pltpu.VMEM)
    near, near_query = pl.pallas_call(
        near_kernel,
        out_shape=(
            jax.ShapeDtypeStruct((4 * own.shape[0], 2 * width), bf16),
            jax.ShapeDtypeStruct((4 * own.shape[0], width), bf16),
        ),
        in_specs=[vmem] * 5,
        out_specs=(vmem, vmem),
        compiler_params=pltpu.CompilerParams(vmem_limit_bytes=8 * 1024 * 1024),
        cost_estimate=pl.CostEstimate(flops=0, bytes_accessed=8 * own.size * 2, transcendentals=0),
    )(own, before, *far_side(before, behind, sides, 0), behind)
    before, behind = ring(near, sides, 1)

    mine = [group_ring(block)]
    second, *_ = lax.optimization_barrier((mine[0], *first_ring))
    mine.append(group_ring(second))
    mine.append(group_ring(mine[1]))
    last = lax.dynamic_slice_in_dim(mine[-1], core * (depth // 2), depth // 2, axis=1)
    shared = [swap_cores(each) for each in mine[:2]]
    last, *shared = lax.optimization_barrier((last, *shared))
    mine.append(group_ring(last))
    far = far_side(before, behind, sides, 1)
    query_ring = ring(near_query, sides, 1)
    *rest, top, bottom, before_query, behind_query = lax.optimization_barrier(
        (*mine[2:], *far, *query_ring)
    )
    weights = near, before, behind, top, bottom
    query_weights = near_query, before_query, behind_query, chip_ring(near_query, sides, 1, 2)
    gathered = [block, *mine, *shared, *[swap_cores(each) for each in rest]]

    rates_all = decay_rate / float(sequence)
    rates = own_columns(rates_all, core)
    amplitude = own_columns(residue * jnp.sqrt(-jnp.expm1(-2.0 * rates_all)), core)
    taps = own_columns(short_taps, core)
    modes = rates.shape[0]
    blocks = 8
    lanes = (width // 128, positions, 128)
    features = depth * groups
    dma = pltpu.SemaphoreType.DMA

    signal, block_ends, end_state = on_device(
        functools.partial(key_value_kernel, groups, sides),
        (
            jax.ShapeDtypeStruct(lanes, f32),
            jax.ShapeDtypeStruct((modes, blocks, width), f32),
            jax.ShapeDtypeStruct((chips, modes, width), f32),
        ),
        [
            pltpu.VMEM((positions + HALO, features), bf16),
            pltpu.VMEM((features, 2 * width), bf16),
            pltpu.VMEM((positions + HALO, 2 * width), f32),
            dma((9,)),
            dma((16,)),
        ],
        4 * positions * features * width,
        20,
        14,
        place, *gathered, *weights, taps, rates,
    )
    states = lax.all_to_all(end_state, ("y", "x"), 0, 0, tiled=True)
    query = on_device(
        functools.partial(query_kernel, groups, sides),
        jax.ShapeDtypeStruct((positions, width), f32),
        [
            pltpu.VMEM((positions + HALO, features), bf16),
            pltpu.VMEM((features, width), bf16),
            pltpu.VMEM((positions + HALO, width), f32),
            dma((9,)),
            dma((16,)),
        ],
        2 * positions * features * width,
        16,
        13,
        place, *gathered, *query_weights, taps,
    )
    gated, out_weight_near = on_device(
        scan_kernel,
        (
            jax.ShapeDtypeStruct((positions, width), bf16),
            jax.ShapeDtypeStruct(out_weight.shape, bf16),
        ),
        [
            pltpu.VMEM((modes, blocks, width), f32),
            pltpu.VMEM(lanes, f32),
            dma((1,)),
        ],
        4 * modes * positions * width,
        16,
        1,
        place, out_weight, signal, query, block_ends, states, rates, amplitude,
    )
    given = swap_cores(gated)
    out_width = out_weight.shape[1] // groups
    half = out_width // 2
    parts = on_device(
        functools.partial(product_kernel, groups),
        (
            jax.ShapeDtypeStruct((positions, half), bf16),
            jax.ShapeDtypeStruct((positions, out_width), bf16),
            jax.ShapeDtypeStruct((positions, out_width), bf16),
            jax.ShapeDtypeStruct((positions, out_width), bf16),
            jax.ShapeDtypeStruct((rows, out_width), bf16),
        ),
        [],
        3 * rows * out_weight.size,
        20,
        0,
        place, gated, given, out_weight_near,
    )
    return reduced(parts, core)


def product_kernel(groups, place, mine, given, weight, far, third, second, first, own):
    core = place[1]
    ahead = 1 - 2 * core
    depth = mine.shape[1]
    count, columns = own.shape
    own_channels = pl.ds(pl.multiple_of(core * depth, depth), depth)
    other_channels = pl.ds(pl.multiple_of((1 - core) * depth, depth), depth)
    own_rows = pl.ds(pl.multiple_of(core * count, count), count)
    other_rows = pl.ds(pl.multiple_of((1 - core) * count, count), count)
    for distance, part in ((4, far), (3, third), (2, second), (1, first), (0, own)):
        group = lax.rem(place[0] + ahead * distance + groups, groups)
        start = group * columns
        if distance == 4:
            start = start + core * part.shape[1]
        to = pl.ds(pl.multiple_of(start, part.shape[1]), part.shape[1])
        wanted = [own_rows] if distance == 0 else [other_rows, own_rows]
        for number, rows in enumerate(wanted):
            total = jnp.dot(mine[rows, :], weight[own_channels, to], preferred_element_type=jnp.float32)
            total += jnp.dot(given[rows, :], weight[other_channels, to], preferred_element_type=jnp.float32)
            part[pl.ds(number * count, count), :] = total.astype(jnp.bfloat16)


def reduced(parts, core):
    far, third, second, first, own = parts
    rows = own.shape[0]
    far = group_ring(far, 2)
    nothing = jnp.zeros_like(far)
    far = jnp.where(
        core == 0,
        jnp.concatenate([far, nothing], axis=1),
        jnp.concatenate([nothing, far], axis=1),
    )
    spans = slice(0, rows), slice(rows, 2 * rows)
    streams = [third[span] for span in spans]
    for part, more in ((second, far), (first, None)):
        for number, span in enumerate(spans):
            arrived = group_ring(streams[number])
            if number:
                arrived, _ = lax.optimization_barrier((arrived, streams[0]))
            streams[number] = part[span] + arrived
            if more is not None:
                streams[number] += more[span]
    other, kept = [group_ring(stream) for stream in streams]
    got = swap_cores(other)
    kept, got = lax.optimization_barrier((kept, got))
    total = own.astype(jnp.float32) + kept.astype(jnp.float32) + got.astype(jnp.float32)
    return total.astype(jnp.bfloat16)


def solution(mesh):
    devices = mesh.devices.reshape(4, 4, 2, 8)
    chips = Mesh(devices, ("y", "x", "core", "chan"))
    seq = ("y", "x", "core")
    placed = (
        P(seq, "chan"),
        P(None, seq, "chan"),
        P(None, None, "chan"),
        P(None, "chan"),
        P(None, "chan"),
        P("chan", None),
    )
    return jax.shard_map(
        shards, mesh=chips, in_specs=placed, out_specs=P(seq, "chan"), check_vma=False
    )
```

```python
import functools

import jax
import jax.numpy as jnp
from jax import lax
from jax.experimental import pallas as pl
from jax.experimental.pallas import tpu as pltpu
from jax.sharding import Mesh, PartitionSpec as P

HALO = 16


def swap_cores(block):
    return lax.ppermute(block, "core", [(0, 1), (1, 0)])


def chip_ring(block, sides, stage, sign):
    ny, nx = sides
    pairs = []
    for y in range(ny):
        for x in range(nx):
            for c in range(2):
                to = (y, (x + sign) % nx) if c == stage else ((y + sign) % ny, x)
                pairs.append(((y * nx + x) * 2 + c, (to[0] * nx + to[1]) * 2 + c))
    return lax.ppermute(block, ("y", "x", "core"), pairs)


def group_ring(block, hops=1):
    n = lax.axis_size("chan")
    pairs = []
    for c in range(2):
        for z in range(n):
            pairs.append((c * n + z, c * n + (z + (1 - 2 * c) * hops) % n))
    return lax.ppermute(block, ("core", "chan"), pairs)


def ring(own, sides, stage):
    return chip_ring(own, sides, stage, 1), chip_ring(own, sides, stage, -1)


def far_side(before, behind, sides, stage):
    half = before.shape[0] // 2
    return chip_ring(before[:half], sides, stage, 1), chip_ring(behind[half:], sides, stage, -1)


def tokens_in_order(place, groups, blocks, gathered, semaphores):
    copies = []
    core = place[1]
    ahead = 1 - 2 * core
    own, mine, partner = blocks
    depth = own.shape[1]
    pieces = [(own, 0, 0, 0)]
    for distance, block in enumerate(mine, 1):
        pieces.append((block, -distance, distance == len(mine), core))
    for distance, block in enumerate(partner, 1):
        pieces.append((block, distance, distance == len(partner), 1 - core))
    for block, offset, halved, side in pieces:
        group = lax.rem(place[0] + offset * ahead + groups, groups)
        column = group * depth
        if halved:
            column = column + side * (depth // 2)
        column = pl.multiple_of(column, 128)
        copies.append(
            pltpu.make_async_copy(
                block,
                gathered.at[:, pl.ds(column, block.shape[1])],
                semaphores.at[len(copies)],
            )
        )
    for copy in copies:
        copy.start()
    return copies


def weights_in_order(place, sides, blocks, gathered, semaphores):
    ny, nx = sides
    core, y, x = place[1], place[2], place[3]
    near, before, behind, *far = blocks
    rows = near.shape[0] // 4
    order = (0, -1, -2, 1)
    pieces = []
    for block, second in ((near, 0), (before, -1), (behind, 1)):
        pieces += [(block, i, first, second) for i, first in enumerate(order)]
    if len(far) == 1:
        pieces += [(far[0], i, first, -2) for i, first in enumerate(order)]
    else:
        pieces += [(far[i // 2], i % 2, first, -2) for i, first in enumerate(order)]
    copies = []
    for block, i, first, second in pieces:
        dx = jnp.where(core == 0, first, second)
        dy = jnp.where(core == 0, second, first)
        chip = lax.rem(y + dy + ny, ny) * nx + lax.rem(x + dx + nx, nx)
        to = pl.multiple_of(chip * rows, 128)
        copies.append(
            pltpu.make_async_copy(
                block.at[pl.ds(i * rows, rows)],
                gathered.at[pl.ds(to, rows)],
                semaphores.at[len(copies)],
            )
        )
    for copy in copies:
        copy.start()
    return copies


def near_kernel(own, before, far_top, far_bottom, behind, key_value, query):
    split = key_value.shape[1]
    row = 0
    for block in (own, before, far_top, far_bottom, behind):
        rows = block.shape[0]
        key_value[pl.ds(row, rows), :] = block[:, pl.ds(0, split)]
        query[pl.ds(row, rows), :] = block[:, pl.ds(split, query.shape[1])]
        row += rows


def take_tokens(refs):
    return refs[0], refs[1:5], refs[5:9]


def project(tokens, weight, projected):
    rows = tokens.shape[0] - HALO
    total = jnp.dot(tokens[...], weight[...], preferred_element_type=jnp.float32)
    total = total.astype(jnp.bfloat16).astype(jnp.float32)
    projected[pl.ds(0, HALO), :] = total[rows:]
    projected[pl.ds(HALO, rows), :] = total[:rows]


def filtered(projected, taps, group, channels, columns):
    rows = projected.shape[0] - HALO
    return sum(
        taps[group, lag : lag + 1, channels] * projected[pl.ds(HALO - lag, rows), columns]
        for lag in range(taps.shape[1])
    )


def query_kernel(groups, sides, place, *refs):
    blocks, weights = take_tokens(refs[:9]), refs[9:13]
    taps, query, tokens, weight, projected, *semaphores = refs[13:]
    copies = tokens_in_order(place, groups, blocks, tokens, semaphores[0])
    copies += weights_in_order(place, sides, weights, weight, semaphores[1])
    for copy in copies:
        copy.wait()
    project(tokens, weight, projected)
    query[...] = filtered(projected, taps, 0, slice(None), slice(None))


def key_value_kernel(groups, sides, place, *refs):
    blocks, weights = take_tokens(refs[:9]), refs[9:14]
    taps, rates, signal, block_ends, end_state, tokens, weight, projected, *semaphores = refs[14:]
    copies = tokens_in_order(place, groups, blocks, tokens, semaphores[0])
    copies += weights_in_order(place, sides, weights, weight, semaphores[1])
    for copy in copies:
        copy.wait()
    project(tokens, weight, projected)
    modes, blocks, width = block_ends.shape
    steps = signal.shape[1] // blocks
    for part in range(width // 128):
        lanes = pl.ds(part * 128, 128)
        key = filtered(projected, taps, 1, lanes, lanes)
        value = filtered(projected, taps, 2, lanes, pl.ds(width + part * 128, 128))
        signal[part] = key * value
        decay = [
            jnp.broadcast_to(jnp.exp(-rates[m : m + 1, lanes]), (blocks, 128)) for m in range(modes)
        ]

        def step(s, states):
            u = signal[part, pl.ds(s, blocks, steps), :]
            return tuple(decay[m] * states[m] + u for m in range(modes))

        zero = jnp.zeros((blocks, 128), jnp.float32)
        states = lax.fori_loop(0, steps, step, (zero,) * modes, unroll=8)
        for m in range(modes):
            block_ends[m, :, lanes] = states[m]
    block_decay = jnp.exp(-rates[...] * float(steps))
    state = block_ends[:, 0, :]
    for b in range(1, blocks):
        state = block_decay * state + block_ends[:, b, :]
    for chip in range(end_state.shape[0]):
        end_state[chip] = state


def scan_kernel(place, out_weight, signal, query, block_ends, states, rates, amplitude, *refs):
    gated, out_weight_near, block_starts, result, semaphore = refs
    copy = pltpu.make_async_copy(out_weight, out_weight_near, semaphore.at[0])
    copy.start()
    modes, blocks, width = block_ends.shape
    steps = signal.shape[1] // blocks
    chip_decay = jnp.exp(-rates[...] * float(steps * blocks))
    state = jnp.zeros((modes, width), jnp.float32)
    for chip in range(states.shape[0] - 1):
        state = jnp.where(chip < place[4], chip_decay * state + states[chip], state)
    block_decay = jnp.exp(-rates[...] * float(steps))
    for b in range(blocks):
        block_starts[:, b, :] = state
        state = block_decay * state + block_ends[:, b, :]
    for part in range(width // 128):
        lanes = pl.ds(part * 128, 128)
        decay = [
            jnp.broadcast_to(jnp.exp(-rates[m : m + 1, lanes]), (blocks, 128)) for m in range(modes)
        ]
        scale = [jnp.broadcast_to(amplitude[m : m + 1, lanes], (blocks, 128)) for m in range(modes)]

        def step(s, states):
            u = signal[part, pl.ds(s, blocks, steps), :]
            states = tuple(decay[m] * states[m] + u for m in range(modes))
            terms = [scale[m] * states[m] for m in range(modes)]
            while len(terms) > 1:
                terms = [a + b for a, b in zip(terms[::2], terms[1::2])]
            result[part, pl.ds(s, blocks, steps), :] = terms[0]
            return states

        states_now = tuple(block_starts[m, :, lanes] for m in range(modes))
        lax.fori_loop(0, steps, step, states_now, unroll=4)
        gated[:, lanes] = (query[:, lanes] * result[part]).astype(jnp.bfloat16)
    copy.wait()


def on_device(kernel, outs, scratch, cost, limit, copied, place, *arrays):
    smem = pl.BlockSpec(memory_space=pltpu.SMEM)
    vmem = pl.BlockSpec(memory_space=pltpu.VMEM)
    hbm = pl.BlockSpec(memory_space=pltpu.HBM)
    kept = [pltpu.with_memory_space_constraint(a, pltpu.HBM) for a in arrays[:copied]]
    return pl.pallas_call(
        kernel,
        out_shape=outs,
        in_specs=[smem] + [hbm] * copied + [vmem] * (len(arrays) - copied),
        out_specs=jax.tree.map(lambda _: vmem, outs),
        scratch_shapes=scratch,
        compiler_params=pltpu.CompilerParams(vmem_limit_bytes=limit * 1024 * 1024),
        cost_estimate=pl.CostEstimate(flops=cost, bytes_accessed=cost // 400, transcendentals=0),
    )(place, *kept, *arrays[copied:])


def shards(tokens, input_weight, short_taps, residue, decay_rate, out_weight):
    f32, bf16 = jnp.float32, jnp.bfloat16
    rows, depth = tokens.shape
    width = input_weight.shape[2] // 2
    groups = lax.axis_size("chan")
    sides = lax.axis_size("y"), lax.axis_size("x")
    chips = sides[0] * sides[1]
    core, z = lax.axis_index("core"), lax.axis_index("chan")
    positions = 2 * rows
    sequence = positions * chips
    y, x = lax.axis_index("y"), lax.axis_index("x")
    place = jnp.stack([z, core, y, x, y * sides[1] + x]).astype(jnp.int32)

    def own_columns(array, owner):
        return lax.dynamic_slice_in_dim(array, owner * width, width, axis=array.ndim - 1)

    def by_core(own, other, axis):
        return jnp.where(
            core == 0,
            jnp.concatenate([own, other], axis=axis),
            jnp.concatenate([other, own], axis=axis),
        )

    other = swap_cores(tokens)
    block = by_core(tokens, other, 0)
    earlier = lax.ppermute(
        block[-HALO:], ("y", "x", "core"), [(i, i + 2) for i in range(2 * chips - 2)]
    )
    block = jnp.concatenate([block, earlier], axis=0)
    kept = own_columns(input_weight, core)
    given, _ = lax.optimization_barrier((own_columns(input_weight, 1 - core), other))
    both = by_core(kept, swap_cores(given), 1)
    own = jnp.concatenate([both[1], both[2], both[0]], axis=1)
    before, behind = first_ring = ring(own, sides, 0)
    vmem = pl.BlockSpec(memory_space=pltpu.VMEM)
    near, near_query = pl.pallas_call(
        near_kernel,
        out_shape=(
            jax.ShapeDtypeStruct((4 * own.shape[0], 2 * width), bf16),
            jax.ShapeDtypeStruct((4 * own.shape[0], width), bf16),
        ),
        in_specs=[vmem] * 5,
        out_specs=(vmem, vmem),
        compiler_params=pltpu.CompilerParams(vmem_limit_bytes=8 * 1024 * 1024),
        cost_estimate=pl.CostEstimate(flops=0, bytes_accessed=8 * own.size * 2, transcendentals=0),
    )(own, before, *far_side(before, behind, sides, 0), behind)
    before, behind = ring(near, sides, 1)

    mine = [group_ring(block)]
    second, *_ = lax.optimization_barrier((mine[0], *first_ring))
    mine.append(group_ring(second))
    mine.append(group_ring(mine[1]))
    last = lax.dynamic_slice_in_dim(mine[-1], core * (depth // 2), depth // 2, axis=1)
    shared = [swap_cores(each) for each in mine[:2]]
    last, *shared = lax.optimization_barrier((last, *shared))
    mine.append(group_ring(last))
    far = far_side(before, behind, sides, 1)
    query_ring = ring(near_query, sides, 1)
    *rest, top, bottom, before_query, behind_query = lax.optimization_barrier(
        (*mine[2:], *far, *query_ring)
    )
    weights = near, before, behind, top, bottom
    query_weights = near_query, before_query, behind_query, chip_ring(near_query, sides, 1, 2)
    gathered = [block, *mine, *shared, *[swap_cores(each) for each in rest]]

    rates_all = decay_rate / float(sequence)
    rates = own_columns(rates_all, core)
    amplitude = own_columns(residue * jnp.sqrt(-jnp.expm1(-2.0 * rates_all)), core)
    taps = own_columns(short_taps, core)
    modes = rates.shape[0]
    blocks = 8
    lanes = (width // 128, positions, 128)
    features = depth * groups
    dma = pltpu.SemaphoreType.DMA

    signal, block_ends, end_state = on_device(
        functools.partial(key_value_kernel, groups, sides),
        (
            jax.ShapeDtypeStruct(lanes, f32),
            jax.ShapeDtypeStruct((modes, blocks, width), f32),
            jax.ShapeDtypeStruct((chips, modes, width), f32),
        ),
        [
            pltpu.VMEM((positions + HALO, features), bf16),
            pltpu.VMEM((features, 2 * width), bf16),
            pltpu.VMEM((positions + HALO, 2 * width), f32),
            dma((9,)),
            dma((16,)),
        ],
        4 * positions * features * width,
        20,
        12,
        place, *gathered, *weights, taps, rates,
    )
    states = lax.all_to_all(end_state, ("y", "x"), 0, 0, tiled=True)
    query = on_device(
        functools.partial(query_kernel, groups, sides),
        jax.ShapeDtypeStruct((positions, width), f32),
        [
            pltpu.VMEM((positions + HALO, features), bf16),
            pltpu.VMEM((features, width), bf16),
            pltpu.VMEM((positions + HALO, width), f32),
            dma((9,)),
            dma((16,)),
        ],
        2 * positions * features * width,
        16,
        13,
        place, *gathered, *query_weights, taps,
    )
    gated, out_weight_near = on_device(
        scan_kernel,
        (
            jax.ShapeDtypeStruct((positions, width), bf16),
            jax.ShapeDtypeStruct(out_weight.shape, bf16),
        ),
        [
            pltpu.VMEM((modes, blocks, width), f32),
            pltpu.VMEM(lanes, f32),
            dma((1,)),
        ],
        4 * modes * positions * width,
        16,
        1,
        place, out_weight, signal, query, block_ends, states, rates, amplitude,
    )
    given = swap_cores(gated)
    out_width = out_weight.shape[1] // groups
    half = out_width // 2
    parts = on_device(
        functools.partial(product_kernel, groups),
        (
            jax.ShapeDtypeStruct((positions, half), bf16),
            jax.ShapeDtypeStruct((positions, out_width), bf16),
            jax.ShapeDtypeStruct((positions, out_width), bf16),
            jax.ShapeDtypeStruct((positions, out_width), bf16),
            jax.ShapeDtypeStruct((rows, out_width), bf16),
        ),
        [],
        3 * rows * out_weight.size,
        20,
        0,
        place, gated, given, out_weight_near,
    )
    return reduced(parts, core)


def product_kernel(groups, place, mine, given, weight, far, third, second, first, own):
    core = place[1]
    ahead = 1 - 2 * core
    depth = mine.shape[1]
    count, columns = own.shape
    own_channels = pl.ds(pl.multiple_of(core * depth, depth), depth)
    other_channels = pl.ds(pl.multiple_of((1 - core) * depth, depth), depth)
    own_rows = pl.ds(pl.multiple_of(core * count, count), count)
    other_rows = pl.ds(pl.multiple_of((1 - core) * count, count), count)
    for distance, part in ((4, far), (3, third), (2, second), (1, first), (0, own)):
        group = lax.rem(place[0] + ahead * distance + groups, groups)
        start = group * columns
        if distance == 4:
            start = start + core * part.shape[1]
        to = pl.ds(pl.multiple_of(start, part.shape[1]), part.shape[1])
        wanted = [own_rows] if distance == 0 else [other_rows, own_rows]
        for number, rows in enumerate(wanted):
            total = jnp.dot(mine[rows, :], weight[own_channels, to], preferred_element_type=jnp.float32)
            total += jnp.dot(given[rows, :], weight[other_channels, to], preferred_element_type=jnp.float32)
            part[pl.ds(number * count, count), :] = total.astype(jnp.bfloat16)


def reduced(parts, core):
    far, third, second, first, own = parts
    rows = own.shape[0]
    far = group_ring(far, 2)
    nothing = jnp.zeros_like(far)
    far = jnp.where(
        core == 0,
        jnp.concatenate([far, nothing], axis=1),
        jnp.concatenate([nothing, far], axis=1),
    )
    spans = slice(0, rows), slice(rows, 2 * rows)
    streams = [third[span] for span in spans]
    for part, more in ((second, far), (first, None)):
        for number, span in enumerate(spans):
            arrived = group_ring(streams[number])
            if number:
                arrived, _ = lax.optimization_barrier((arrived, streams[0]))
            streams[number] = part[span] + arrived
            if more is not None:
                streams[number] += more[span]
    other, kept = [group_ring(stream) for stream in streams]
    got = swap_cores(other)
    kept, got = lax.optimization_barrier((kept, got))
    total = own.astype(jnp.float32) + kept.astype(jnp.float32) + got.astype(jnp.float32)
    return total.astype(jnp.bfloat16)


def solution(mesh):
    devices = mesh.devices.reshape(4, 4, 2, 8)
    chips = Mesh(devices, ("y", "x", "core", "chan"))
    seq = ("y", "x", "core")
    placed = (
        P(seq, "chan"),
        P(None, seq, "chan"),
        P(None, None, "chan"),
        P(None, "chan"),
        P(None, "chan"),
        P("chan", None),
    )
    return jax.shard_map(
        shards, mesh=chips, in_specs=placed, out_specs=P(seq, "chan"), check_vma=False
    )
```
